32 devices in a mesh: grp: 2 (over x), gx: 16 (over z, y, core).
Axes of the slice: x: 2, y: 2, z: 4, core: 2. Of those that a mesh axis runs over, the one named last changes fastest.
Arguments:
- point_fraction: bfloat16 [512, 3, 128], P(('grp', 'gx')), parts along dimension 0, may hold values from 0 to 1
- point_features: bfloat16 [512, 8, 128], P(('grp', 'gx')), parts along dimension 0, may hold values from -6 to 6
- base_cell: int32 [512, 128], P(('grp', 'gx')), parts along dimension 0, may hold values from 0 to 3966, as said below
- corner_bits: int32 [512, 128], P(('grp', 'gx')), parts along dimension 0, may hold values from 0 to 255
- owner_map: int32 [512, 1], P(('grp', 'gx')), parts along dimension 0, may hold values from 0 to 15; in each aligned block of 16 rows (0 to 15, 16 to 31, ...) at most 2 rows name the same one
- cotangent: bfloat16 [512, 4, 128], P(('grp', 'gx')), parts along dimension 0, may hold values from -6 to 6
- lift_weight: bfloat16 [64, 8], replicated, may hold values from -2 to 2
- encode_inner: float32 [64, 3], replicated, may hold values from -6 to 6
- encode_bias: float32 [64], replicated, may hold values from -4 to 4
- encode_outer: bfloat16 [64, 64], replicated, may hold values from -0.75 to 0.75
- stencil_weight: bfloat16 [27, 64, 64], replicated, may hold values from -0.15625 to 0.15625
- stencil_bias: float32 [64], replicated, may hold values from -3 to 3
- decode_inner: float32 [64, 3], replicated, may hold values from -6 to 6
- decode_bias: float32 [64], replicated, may hold values from -4 to 4
- decode_outer: bfloat16 [64, 64], replicated, may hold values from -0.75 to 0.75
- output_weight: bfloat16 [4, 64], replicated, may hold values from -0.75 to 0.75
Outputs:
- predictions: bfloat16 [512, 4, 128], P(('grp', 'gx')), parts along dimension 0
- stencil_grad: float32 [128, 1728], P(('grp', 'gx')), parts along dimension 0
The draws below stay inside these ranges and needn't reach their ends.
There are 2 independent parts, one for each index of `grp`. The reference program is written for one: setup_inputs(seed, part) draws one part's arguments, and reference() takes and returns one part's arrays. A program takes and returns all parts, laid end to end along the dimension named above; an argument that names none is the same for every part. Nothing has to cross between parts.
Inputs may be any that keep to these rules, and one draw needn't show every extreme that they name: `base_cell`: flat index x * 16 * 128 + y * 128 + z with x < 2, y < 15, z < 127. `corner_bits`: bit j marks corner j of the point's cell as within the radius. `owner_map`: among the blocks of one device at most 2 have the same owner; some device has exactly 2 blocks with one owner.
All inputs are finite; a program needn't handle non-finite values.
Results may differ from the reference program's by a relative error of at most 0.02.
Values may be sent and summed in bfloat16 or wider, within the bound.
A program may use at most 64 MiB of HBM per device.

```python
import math
import jax
import jax.numpy as jnp
import numpy as np
from jax import lax

CH = 64
PF = 8
KH = 64
OUTC = 4
BLK = 128
CAP = 2
GXD = 2
GY = 16
GZ = 128
NB = 16
NBLK = 256
NX = 32
N_GX = 16


def draw_base_cell(key, part):
    key = jax.random.fold_in(key, 11)
    key_x, key_y, key_z = jax.random.split(key, 3)
    shape = (NBLK, BLK)
    plane = jax.random.randint(key_x, shape, 0, GXD)
    across = jax.random.randint(key_y, shape, 0, GY - 1)
    height = jax.random.randint(key_z, shape, 0, GZ - 1)
    return (plane * (GY * GZ) + across * GZ + height).astype(jnp.int32)


def touch_ends(drawn, own_key, least, high):
    longest = drawn.shape.index(max(drawn.shape))
    spots = []
    for shift in (0, 1):
        where = [jax.random.randint(jax.random.fold_in(own_key, axis), (), 0, length) for axis, length in enumerate(drawn.shape)]
        where[longest] = (where[longest] + shift) % drawn.shape[longest]
        spots.append(tuple(where))
    return drawn.at[spots[0]].set(least).at[spots[1]].set(high)


def levels(key, shape, pieces, smallest, largest):
    factor_of, own = 1.0, jax.random.fold_in(key, 6)
    for dim, blocks in pieces:
        heights = jnp.exp(jax.random.uniform(jax.random.fold_in(own, dim), (blocks,), jnp.float32, smallest / len(pieces), largest / len(pieces)))
        factor_of = factor_of * jnp.repeat(heights, shape[dim] // blocks).reshape([-1 if axis == dim else 1 for axis in range(len(shape))])
    return factor_of


def assign_block(rng, own, number, rows, count, top, limit, slope):
    order = jax.random.permutation(rng, count)
    heavy_load, usual = shares(count, rows * top, limit, slope, True), shares(count, rows * top, limit, slope, False)
    places = jnp.arange(count)

    def named(sizes, rotation):
        used = int((sizes > 0).sum())
        fixed = max(1, used // 4)
        shifted = fixed + (places - fixed + rotation * (used - fixed)) % max(1, count - fixed)
        return jnp.zeros((count,), jnp.int32).at[order[jnp.where(places < fixed, places, shifted)]].set(jnp.asarray(sizes, jnp.int32))

    sizes = jnp.where(number % 4 == 0, named(heavy_load, number // 4), named(usual, number - number // 4 - 1))
    mixed = jax.random.permutation(jax.random.fold_in(own, 3), count)
    giver, sink = mixed[0:count // 2 * 2:2], mixed[1:count // 2 * 2:2]
    margin = jnp.minimum(sizes[giver] - 1, limit - sizes[sink]) // 2
    margin = jnp.where((giver == order[0]) | (sink == order[0]) | (sizes[sink] == 0), 0, jnp.maximum(margin, 0))
    shifted = jax.random.randint(jax.random.fold_in(own, 4), (count // 2,), 0, 1 << 20) % (margin + 1)
    sizes = sizes.at[giver].add(-shifted).at[sink].add(shifted)
    items = jnp.searchsorted(jnp.cumsum(sizes), jnp.arange(rows * top), side="right").astype(jnp.int32)
    grid = items.reshape(top, rows).T
    grid = grid[jax.random.permutation(jax.random.fold_in(own, 1), rows)]
    rotation = jax.random.randint(jax.random.fold_in(own, 2), (rows, 1), 0, top)
    return jnp.take_along_axis(grid, (jnp.arange(top)[None, :] + rotation) % top, axis=1)


def shares(amount, total, bound, skew, full):
    loads = [(1 << 20) // math.isqrt(rank ** skew) + 1 for rank in range(1, amount + 1)]
    largest = bound if full else min(bound, max(-(-total // amount), total * loads[0] // sum(loads)))
    least = 1 if total - largest >= amount - 1 else 0
    given, surplus = [largest] + [least] * (amount - 1), total - largest - least * (amount - 1)
    while surplus > 0:
        free = [i for i in range(1, amount) if given[i] < largest] or [i for i in range(1, amount) if given[i] < bound]
        mass, remaining = sum([loads[i] for i in free]), surplus
        for i in free:
            more = min(bound - given[i], max(1, remaining * loads[i] // mass), surplus)
            given[i] = given[i] + more
            surplus = surplus - more
    return np.array(given)


def bell_draw(stream_key, shape, deviation, limit, pieces=(), kind=jnp.bfloat16):
    values = deviation * jax.random.normal(stream_key, shape, jnp.float32)
    if pieces:
        values = values * levels(stream_key, shape, pieces, -0.22, 0.18)
    return jnp.clip(values, -limit, limit).astype(kind)


def setup_inputs(seed: int = 0, part: int = 0) -> dict:
    splits = jax.random.split(jax.random.key(seed), 17)
    own_keys = jax.random.split(jax.random.fold_in(splits[16], part), 17)
    point_fraction = jnp.clip(1.0 * jax.random.uniform(own_keys[0], (NBLK, 3, BLK), jnp.float32) ** levels(own_keys[0], (NBLK, 3, BLK), ((0, 16),), -0.2, 0.2), 0.0, 1.0).astype(jnp.bfloat16)
    point_features = bell_draw(own_keys[1], (NBLK, PF, BLK), 1.0, 6.0, ((0, 16),))
    base_cell = draw_base_cell(jax.random.fold_in(jax.random.fold_in(splits[16], part), 71), part)
    corner_bits = touch_ends(jax.random.randint(own_keys[3], (NBLK, BLK), 0, 256), jax.random.fold_in(own_keys[3], 1), 0, 255).astype(jnp.int32)
    owner_map_keys = jax.random.split(jax.random.fold_in(own_keys[4], 1), NBLK // NB)
    owner_map_turns = jax.random.permutation(jax.random.fold_in(own_keys[4], 3), NBLK // NB)
    owner_map = jax.vmap(lambda own, number: assign_block(jax.random.fold_in(own_keys[4], 2), own, number, NB, N_GX, 1, CAP, 2))(owner_map_keys, owner_map_turns).reshape((NBLK, 1))
    cotangent = bell_draw(own_keys[5], (NBLK, OUTC, BLK), 1.0, 6.0, ((0, 16),))
    lift_weight = bell_draw(splits[6], (CH, PF), PF ** -0.5, 2.0)
    encode_inner = bell_draw(splits[7], (KH, 3), 1.5, 6.0, (), jnp.float32)
    encode_bias = bell_draw(splits[8], (KH,), 1.0, 4.0, (), jnp.float32)
    encode_outer = bell_draw(splits[9], (CH, KH), KH ** -0.5, 0.75)
    stencil_weight = bell_draw(splits[10], (27, CH, CH), (27 * CH) ** -0.5, 0.15625)
    stencil_bias = bell_draw(splits[11], (CH,), 0.5, 3.0, (), jnp.float32)
    decode_inner = bell_draw(splits[12], (KH, 3), 1.5, 6.0, (), jnp.float32)
    decode_bias = bell_draw(splits[13], (KH,), 1.0, 4.0, (), jnp.float32)
    decode_outer = bell_draw(splits[14], (CH, KH), KH ** -0.5, 0.75)
    output_weight = bell_draw(splits[15], (OUTC, CH), CH ** -0.5, 0.75)
    return dict(point_fraction=point_fraction, point_features=point_features, base_cell=base_cell, corner_bits=corner_bits, owner_map=owner_map, cotangent=cotangent, lift_weight=lift_weight, encode_inner=encode_inner, encode_bias=encode_bias, encode_outer=encode_outer, stencil_weight=stencil_weight, stencil_bias=stencil_bias, decode_inner=decode_inner, decode_bias=decode_bias, decode_outer=decode_outer, output_weight=output_weight)


def smooth(values):
    return 0.5 * values * (1.0 + jnp.tanh(0.7978845608 * (values + 0.044715 * values * values * values)))


def smooth_slope(values):
    return jax.jvp(smooth, (values,), (jnp.ones_like(values),))[1]


def corner_table():
    corner = jnp.arange(8, dtype=jnp.int32)
    return jnp.stack([corner // 4, corner // 2 % 2, corner % 2])


def corner_offsets():
    shifts = corner_table()
    return (shifts[0] * (GY * GZ) + shifts[1] * GZ + shifts[2]).astype(jnp.int32)


def corner_live(bit_words):
    corner = jnp.arange(8, dtype=jnp.int32)
    return (jnp.right_shift(bit_words[None], corner[:, None, None]) & 1).astype(jnp.float32)


def kernel_values(fraction, first_layer, offset_bias, second_layer):
    shifts = corner_table().astype(jnp.float32)
    placed = jnp.transpose(fraction.astype(jnp.float32), (1, 0, 2))
    displace = shifts[:, :, None, None] - placed[:, None]
    hidden_pre = (first_layer[:, 0, None, None, None] * displace[0]
                  + first_layer[:, 1, None, None, None] * displace[1]
                  + first_layer[:, 2, None, None, None] * displace[2]
                  + offset_bias[:, None, None, None])
    hidden = smooth(hidden_pre).astype(jnp.bfloat16)
    return jnp.einsum('ck,kjgp->cjgp', second_layer.astype(jnp.float32), hidden.astype(jnp.float32)).astype(jnp.bfloat16)


def stencil(source, weight, offset_bias, planes):
    padded = jnp.pad(source, ((0, 0), (0, 0), (1, 1), (1, 1))).astype(jnp.float32)
    running = jnp.zeros((source.shape[0], planes, GY, GZ), jnp.float32)
    for offset in range(27):
        along_x, along_y, along_z = offset // 9, offset // 3 % 3, offset % 3
        window = padded[:, along_x:along_x + planes, along_y:along_y + GY, along_z:along_z + GZ]
        running = running + jnp.einsum('oc,cxyz->oxyz', weight[offset].astype(jnp.float32), window)
    return running + offset_bias[:, None, None, None]


def stencil_terms(grad_pre, source, planes):
    padded = jnp.pad(source, ((0, 0), (0, 0), (1, 1), (1, 1))).astype(jnp.float32)
    upstream = grad_pre.astype(jnp.float32)
    partial_terms = []
    for offset in range(27):
        along_x, along_y, along_z = offset // 9, offset // 3 % 3, offset % 3
        window = padded[:, along_x:along_x + planes, along_y:along_y + GY, along_z:along_z + GZ]
        partial_terms.append(jnp.einsum('oxyz,cxyz->oc', upstream, window))
    stacked = jnp.stack(partial_terms, axis=1)
    return stacked.reshape(stacked.shape[0], -1)


def reference(point_fraction, point_features, base_cell, corner_bits, owner_map, cotangent, lift_weight,
              encode_inner, encode_bias, encode_outer, stencil_weight, stencil_bias, decode_inner, decode_bias,
              decode_outer, output_weight):
    channels = lift_weight.shape[0]
    block_group = 16
    rounds = NBLK // block_group
    slab_cells = GXD * GY * GZ
    total_cells = (NX + 1) * GY * GZ
    offsets = corner_offsets()

    def grouped(values):
        return values.reshape((rounds, block_group) + values.shape[1:])

    portions = (grouped(point_fraction), grouped(point_features), grouped(base_cell), grouped(corner_bits),
                grouped(owner_map[:, 0]), grouped(cotangent))

    def cells_of(base_ids, owners):
        return (owners[None, :, None] * slab_cells + base_ids[None] + offsets[:, None, None]).astype(jnp.int32)

    def encode_step(grid_sum, portion):
        fraction, features, base_ids, bit_words, owners, unused = portion
        kernel_out = kernel_values(fraction, encode_inner, encode_bias, encode_outer)
        lifted = jnp.einsum('cf,gfp->cgp', lift_weight.astype(jnp.float32), features.astype(jnp.float32)).astype(jnp.bfloat16)
        corner_on = corner_live(bit_words)
        cell_ids = cells_of(base_ids, owners)
        contribution = kernel_out.astype(jnp.float32) * lifted.astype(jnp.float32)[:, None] * corner_on[None]
        return grid_sum.at[:, cell_ids.reshape(-1)].add(contribution.reshape(channels, -1)), None

    grid_sum, unused = lax.scan(encode_step, jnp.zeros((channels, total_cells), jnp.float32), portions)
    latent_in = grid_sum.reshape(channels, NX + 1, GY, GZ)[:, :NX].astype(jnp.bfloat16)
    faced = jnp.pad(latent_in, ((0, 0), (1, 1), (0, 0), (0, 0)))
    stencil_pre = stencil(faced, stencil_weight, stencil_bias, NX)
    latent_out = smooth(stencil_pre).astype(jnp.bfloat16)
    latent_flat = jnp.concatenate([latent_out, jnp.zeros((channels, 1, GY, GZ), jnp.bfloat16)], axis=1).reshape(channels, -1)

    def decode_step(grad_sum, portion):
        fraction, features, base_ids, bit_words, owners, cotangent_in = portion
        kernel_out = kernel_values(fraction, decode_inner, decode_bias, decode_outer)
        corner_on = corner_live(bit_words)
        cell_ids = cells_of(base_ids, owners)
        gathered = jnp.take(latent_flat, cell_ids.reshape(-1), axis=1).reshape(kernel_out.shape)
        queried = jnp.sum(kernel_out.astype(jnp.float32) * gathered.astype(jnp.float32) * corner_on[None], axis=1).astype(jnp.bfloat16)
        predicted = jnp.einsum('oc,cgp->gop', output_weight.astype(jnp.float32), queried.astype(jnp.float32)).astype(jnp.bfloat16)
        grad_query = jnp.einsum('oc,gop->cgp', output_weight.astype(jnp.float32), cotangent_in.astype(jnp.float32)).astype(jnp.bfloat16)
        contribution = kernel_out.astype(jnp.float32) * grad_query.astype(jnp.float32)[:, None] * corner_on[None]
        return grad_sum.at[:, cell_ids.reshape(-1)].add(contribution.reshape(channels, -1)), predicted

    grad_sum, predicted = lax.scan(decode_step, jnp.zeros((channels, total_cells), jnp.float32), portions)
    grad_out = grad_sum.reshape(channels, NX + 1, GY, GZ)[:, :NX]
    grad_pre = (grad_out * smooth_slope(stencil_pre)).astype(jnp.bfloat16)
    stencil_grad = stencil_terms(grad_pre, faced, NX)
    return predicted.reshape(NBLK, OUTC, BLK), stencil_grad
```

```python
import functools

import jax
import jax.numpy as jnp
from jax import lax
from jax.experimental import pallas as pl
from jax.experimental.pallas import tpu as pltpu
from jax.sharding import PartitionSpec as P

CAP = 2
GXD = 2
GY = 16
GZ = 128
PLANE = GY * GZ
BASE = GXD * PLANE
EXT = (GXD + 1) * PLANE
PADDED = (GY + 2) * GZ
GROUP = 4
CHUNK = GROUP * 128
TILE = 256
BF = jnp.bfloat16
F32 = jnp.float32
NT = (((1,), (1,)), ((), ()))
VMEM_LIMIT = 56 * 1024 * 1024


def smooth(v):
    return 0.5 * v * (1.0 + jnp.tanh(v * (0.7978845608 + (0.7978845608 * 0.044715) * (v * v))))


def smooth_slope(v):
    square = v * v
    t = jnp.tanh(v * (0.7978845608 + (0.7978845608 * 0.044715) * square))
    inner = 0.7978845608 + (3.0 * 0.7978845608 * 0.044715) * square
    return 0.5 * (1.0 + t) + 0.5 * v * (1.0 - t * t) * inner


def point_chunk(order_ref, pts_ref, chunk):
    return jnp.concatenate(
        [pts_ref[order_ref[chunk * GROUP + q]] for q in range(GROUP)], axis=1
    )


def cells_of(points):
    return (points[16:17] * GZ + points[17:18]).astype(jnp.int32)


def scatter_kernel(keep, order_ref, count_ref, pts_ref, value_w_ref, inner_ref, bias_ref, outer_ref, *rest):
    if keep:
        grid_ref, kept_ref, acc_ref, part_ref = rest
    else:
        grid_ref, acc_ref, part_ref = rest
    channels = outer_ref.shape[0]
    chunks = (count_ref[0] + (GROUP - 1)) // GROUP
    acc_ref[...] = jnp.zeros_like(acc_ref)
    inner = inner_ref[...]

    @pl.loop(0, chunks)
    def _(chunk):
        points = point_chunk(order_ref, pts_ref, chunk)
        values = jnp.dot(value_w_ref[...], points.astype(BF), preferred_element_type=F32)
        values = values.astype(BF).astype(F32)
        cell = cells_of(points)
        bits = points[18:19].astype(jnp.int32)
        base = bias_ref[...] - (
            inner[:, 0:1] * points[12:13] + inner[:, 1:2] * points[13:14] + inner[:, 2:3] * points[14:15]
        )
        for j in range(8):
            shift = inner[:, 0:1] * (j // 4) + inner[:, 1:2] * (j // 2 % 2) + inner[:, 2:3] * (j % 2)
            hidden = smooth(base + shift).astype(BF)
            out = jnp.dot(outer_ref[...], hidden, preferred_element_type=F32)
            live = ((bits >> j) & 1).astype(F32)
            out = (out * live).astype(BF)
            if keep:
                kept_ref[chunk, j * channels : (j + 1) * channels, :] = out
            part_ref[j * channels : (j + 1) * channels, :] = (out.astype(F32) * values).astype(BF)

        @pl.loop(0, BASE // TILE)
        def _(t):
            start = pl.multiple_of(t * TILE, TILE)
            ids = lax.broadcasted_iota(jnp.int32, (TILE, CHUNK), 0) + start
            hot = jnp.where(ids == cell, 1.0, 0.0).astype(BF)
            acc_ref[:, pl.ds(start, TILE)] += lax.dot_general(
                part_ref[...], hot, NT, preferred_element_type=F32
            )

    for row in range((GXD + 1) * GY):
        halves = [None, None]
        for j in range(8):
            source = row - (j // 4) * GY - j // 2 % 2
            if 0 <= source < GXD * GY:
                piece = acc_ref[j * channels : (j + 1) * channels, source * GZ : (source + 1) * GZ]
                have = halves[j % 2]
                halves[j % 2] = piece if have is None else have + piece
        total = halves[0] + pltpu.roll(halves[1], 1, 1)
        grid_ref[:, row * GZ : (row + 1) * GZ] = total.astype(grid_ref.dtype)


def scatter_points(order, count, pts, value_w, inner, bias, outer, keep):
    channels = outer.shape[0]
    slots = pts.shape[0]
    smem = pl.BlockSpec(memory_space=pltpu.SMEM)
    vmem = pl.BlockSpec(memory_space=pltpu.VMEM)
    shapes = [jax.ShapeDtypeStruct((channels, EXT), F32 if keep else BF)]
    if keep:
        shapes.append(jax.ShapeDtypeStruct((slots // GROUP, 8 * channels, CHUNK), BF))
    return pl.pallas_call(
        functools.partial(scatter_kernel, keep),
        out_shape=shapes,
        in_specs=[smem, smem] + [vmem] * 5,
        out_specs=[vmem] * len(shapes),
        scratch_shapes=[
            pltpu.VMEM((8 * channels, BASE), F32),
            pltpu.VMEM((8 * channels, CHUNK), BF),
        ],
        compiler_params=pltpu.CompilerParams(vmem_limit_bytes=VMEM_LIMIT),
        cost_estimate=pl.CostEstimate(
            flops=2 * 8 * channels * BASE * slots * 64, bytes_accessed=4 << 20, transcendentals=0
        ),
    )(order, count, pts, value_w, inner, bias, outer)


def level_kernel(
    order_ref, count_ref, edge_ref, pts_ref, own_ref, left_ref, right_ref, grad_ref, kept_ref,
    weight_ref, bias_ref, out_w_ref, pred_ref, sg_ref, lz_ref, pre_ref, lat_ref, l8_ref, hot_ref,
    gp_ref, win_ref, sum_ref,
):
    channels = own_ref.shape[0]
    inside = jnp.where(edge_ref[0] > 0, 0.0, 1.0).astype(F32)
    z = lax.broadcasted_iota(jnp.int32, (channels, PLANE), 1) % GZ
    first, last = z == 0, z == GZ - 1
    lz_ref[...] = jnp.zeros_like(lz_ref)

    def put_plane(index, plane):
        start = index * PADDED + GZ
        lz_ref[channels : 2 * channels, start : start + PLANE] = plane.astype(BF)
        below = jnp.where(first, 0.0, pltpu.roll(plane, 1, 1))
        above = jnp.where(last, 0.0, pltpu.roll(plane, PLANE - 1, 1))
        lz_ref[0:channels, start : start + PLANE] = below.astype(BF)
        lz_ref[2 * channels :, start : start + PLANE] = above.astype(BF)

    def own(k):
        return own_ref[:, k * PLANE : (k + 1) * PLANE].astype(F32)

    put_plane(0, left_ref[:, 0:PLANE].astype(F32))
    put_plane(1, own(0) + left_ref[:, PLANE:].astype(F32))
    put_plane(2, own(1))
    put_plane(3, (own(2) + right_ref[:, 0:PLANE].astype(F32)) * inside)
    put_plane(4, right_ref[:, PLANE:].astype(F32))

    for x in range(3):
        total = None
        for a in range(3):
            start = (x + a) * PADDED
            terms = jnp.dot(
                weight_ref[a * 3 * channels : (a + 1) * 3 * channels, :],
                lz_ref[:, start : start + PADDED],
                preferred_element_type=F32,
            )
            for e in range(3):
                piece = terms[e * channels : (e + 1) * channels, e * GZ : e * GZ + PLANE]
                total = piece if total is None else total + piece
        pre = total + bias_ref[...]
        pre_ref[x] = pre
        out = smooth(pre)
        if x == 2:
            out = out * inside
        lat_ref[0, :, x * PLANE : (x + 1) * PLANE] = out.astype(BF)
        lat_ref[1, :, x * PLANE : (x + 1) * PLANE] = pltpu.roll(out, PLANE - 1, 1).astype(BF)
    lat_ref[:, :, 3 * PLANE :] = jnp.zeros((2, channels, GZ), BF)
    for j in range(8):
        start = (j // 4) * PLANE + (j // 2 % 2) * GZ
        l8_ref[j * channels : (j + 1) * channels, :] = lat_ref[j % 2, :, start : start + BASE]

    pred_ref[...] = jnp.zeros_like(pred_ref)
    chunks = (count_ref[0] + (GROUP - 1)) // GROUP

    @pl.loop(0, chunks)
    def _(chunk):
        cell = cells_of(point_chunk(order_ref, pts_ref, chunk))

        @pl.loop(0, BASE // TILE)
        def _(t):
            start = pl.multiple_of(t * TILE, TILE)
            ids = lax.broadcasted_iota(jnp.int32, (TILE, CHUNK), 0) + start
            hot_ref[pl.ds(start, TILE), :] = jnp.where(ids == cell, 1.0, 0.0).astype(BF)

        queried = None
        for j in range(8):
            rows = slice(j * channels, (j + 1) * channels)
            if j % 4 == 0:
                wide = jnp.dot(
                    l8_ref[j * channels : (j + 4) * channels, :], hot_ref[...], preferred_element_type=F32
                )
            got = wide[(j % 4) * channels : (j % 4 + 1) * channels]
            term = got * kept_ref[chunk, rows, :].astype(F32)
            queried = term if queried is None else queried + term
        predicted = jnp.dot(out_w_ref[...], queried.astype(BF), preferred_element_type=F32)
        for q in range(GROUP):
            pred_ref[order_ref[chunk * GROUP + q]] = predicted[:, q * 128 : (q + 1) * 128]

    for x in range(3):
        grad = grad_ref[:, x * PLANE : (x + 1) * PLANE] * smooth_slope(pre_ref[x])
        if x == 2:
            grad = grad * inside
        gp_ref[0:channels, :] = jnp.where(last, 0.0, pltpu.roll(grad, PLANE - 1, 1)).astype(BF)
        gp_ref[channels : 2 * channels, :] = grad.astype(BF)
        gp_ref[2 * channels :, :] = jnp.where(first, 0.0, pltpu.roll(grad, 1, 1)).astype(BF)
        for k in range(9):
            start = (x + k // 3) * PADDED + (k % 3) * GZ
            win_ref[k * channels : (k + 1) * channels, :] = lz_ref[
                channels : 2 * channels, start : start + PLANE
            ]
        term = lax.dot_general(gp_ref[...], win_ref[...], NT, preferred_element_type=F32)
        if x == 0:
            sum_ref[...] = term
        else:
            sum_ref[...] += term
    for k in range(27):
        f, place = k % 3, k // 3
        sg_ref[:, k * channels : (k + 1) * channels] = sum_ref[
            f * channels : (f + 1) * channels, place * channels : (place + 1) * channels
        ].astype(BF)


def level(order, count, edge, pts, own, left, right, grad, kept, weight, bias, out_w):
    channels = own.shape[0]
    slots = pts.shape[0]
    smem = pl.BlockSpec(memory_space=pltpu.SMEM)
    vmem = pl.BlockSpec(memory_space=pltpu.VMEM)
    return pl.pallas_call(
        level_kernel,
        out_shape=[
            jax.ShapeDtypeStruct((slots, out_w.shape[0], 128), F32),
            jax.ShapeDtypeStruct((channels, 27 * channels), BF),
        ],
        in_specs=[smem] * 3 + [vmem] * 9,
        out_specs=[vmem] * 2,
        scratch_shapes=[
            pltpu.VMEM((3 * channels, 5 * PADDED), BF),
            pltpu.VMEM((3, channels, PLANE), F32),
            pltpu.VMEM((2, channels, EXT + GZ), BF),
            pltpu.VMEM((8 * channels, BASE), BF),
            pltpu.VMEM((BASE, CHUNK), BF),
            pltpu.VMEM((3 * channels, PLANE), BF),
            pltpu.VMEM((9 * channels, PLANE), BF),
            pltpu.VMEM((3 * channels, 9 * channels), F32),
        ],
        compiler_params=pltpu.CompilerParams(vmem_limit_bytes=VMEM_LIMIT),
    )(order, count, edge, pts, own, left, right, grad, kept, weight, bias, out_w)


def shards(
    point_fraction, point_features, base_cell, corner_bits, owner_map, cotangent, lift_weight,
    encode_inner, encode_bias, encode_outer, stencil_weight, stencil_bias, decode_inner,
    decode_bias, decode_outer, output_weight,
):
    devices = lax.axis_size("gx")
    me = lax.axis_index("gx")
    slots = devices * CAP
    channels = lift_weight.shape[0]
    target = owner_map[:, 0]
    held = target.shape[0]
    matching = target[:, None] == target[None, :]
    earlier = jnp.arange(held)[None, :] < jnp.arange(held)[:, None]
    ranking = jnp.sum(jnp.logical_and(matching, earlier), axis=1)
    places = target * CAP + ranking
    pick = (places[:, None] == jnp.arange(slots)[None, :]).astype(BF)

    packed = jnp.concatenate(
        [
            point_features,
            cotangent,
            point_fraction,
            jnp.zeros((held, 1, 128), BF),
            (base_cell // GZ).astype(BF)[:, None],
            (base_cell % GZ).astype(BF)[:, None],
            corner_bits.astype(BF)[:, None],
            jnp.ones((held, 1, 128), BF),
            jnp.zeros((held, 4, 128), BF),
        ],
        axis=1,
    ).reshape(held, -1)
    sent = jnp.dot(pick.T, packed, preferred_element_type=F32).astype(BF)
    pts = lax.all_to_all(sent, "gx", split_axis=0, concat_axis=0, tiled=True)
    pts = pts.reshape(slots, 24, 128).astype(F32)

    active = pts[:, 19, 0] > 0.5
    before = jnp.arange(slots)[None, :] < jnp.arange(slots)[:, None]
    count = jnp.sum(active.astype(jnp.int32))
    ahead_on = jnp.sum((before & active[None, :]).astype(jnp.int32), axis=1)
    ahead_off = jnp.sum((before & ~active[None, :]).astype(jnp.int32), axis=1)
    place = jnp.where(active, ahead_on, count + ahead_off)
    order = jnp.sum(
        jnp.where(place[None, :] == jnp.arange(slots)[:, None], jnp.arange(slots)[None, :], 0), axis=1
    ).astype(jnp.int32)
    count = count.reshape(1)
    edge = (me == devices - 1).astype(jnp.int32).reshape(1)

    lift24 = jnp.pad(lift_weight, ((0, 0), (0, 24 - lift_weight.shape[1])))
    query24 = jnp.pad(output_weight.T, ((0, 0), (8, 12)))
    (own,) = scatter_points(
        order, count, pts, lift24, encode_inner, encode_bias[:, None], encode_outer, False
    )
    up = [(i, i + 1) for i in range(devices - 1)]
    down = [(i + 1, i) for i in range(devices - 1)]
    left = lax.ppermute(own[:, PLANE:], "gx", up)
    right = lax.ppermute(own[:, :BASE], "gx", down)
    grad, kept = scatter_points(
        order, count, pts, query24, decode_inner, decode_bias[:, None], decode_outer, True
    )
    weight = (
        stencil_weight.reshape(9, 3, channels, channels)
        .transpose(0, 2, 1, 3)
        .reshape(9 * channels, 3 * channels)
    )
    out_w = jnp.pad(output_weight, ((0, 4), (0, 0)))
    predicted, terms = level(
        order, count, edge, pts, own, left, right, grad, kept, weight, stencil_bias[:, None], out_w
    )
    outc = output_weight.shape[0]
    predicted = predicted[:, :outc].astype(BF).reshape(devices, -1)
    payload = jnp.concatenate([predicted, terms.reshape(devices, -1)], axis=1)
    back = lax.all_to_all(payload, "gx", split_axis=0, concat_axis=0, tiled=True)
    split = CAP * outc * 128
    returned = back[:, :split].reshape(slots, outc * 128)
    answer = jnp.dot(pick, returned, preferred_element_type=F32).astype(BF).reshape(held, outc, 128)
    stencil_grad = jnp.sum(back[:, split:].astype(F32), axis=0).reshape(-1, 27 * channels)
    return answer, stencil_grad


def solution(mesh):
    points = P(("grp", "gx"), None, None)
    flat = P(("grp", "gx"), None)
    return jax.shard_map(
        shards,
        mesh=mesh,
        in_specs=(points, points, flat, flat, flat, points) + (P(),) * 10,
        out_specs=(points, flat),
        check_vma=False,
    )
```

```python
import jax
import jax.numpy as jnp
from jax import lax
from jax.experimental import pallas as pl
from jax.experimental.pallas import tpu as pltpu
from jax.sharding import PartitionSpec as P

CAP = 2
GXD = 2
GY = 16
GZ = 128
PLANE = GY * GZ
BASE = GXD * PLANE
EXT = (GXD + 1) * PLANE
PADDED = (GY + 2) * GZ
UNROLL = 16
BF = jnp.bfloat16
F32 = jnp.float32
NT = (((1,), (1,)), ((), ()))
VMEM_LIMIT = 60 * 1024 * 1024


def smooth(v):
    return 0.5 * v * (1.0 + jnp.tanh(v * (0.7978845608 + (0.7978845608 * 0.044715) * (v * v))))


def smooth_slope(v):
    square = v * v
    t = jnp.tanh(v * (0.7978845608 + (0.7978845608 * 0.044715) * square))
    inner = 0.7978845608 + (3.0 * 0.7978845608 * 0.044715) * square
    return 0.5 * (1.0 + t) + 0.5 * v * (1.0 - t * t) * inner


def scatter_kernel(
    order_ref, count_ref, cells_ref, pts_ref, lift_ref, query_ref, *rest
):
    nets, (own_ref, grad_ref, kept_ref, acc0_ref, acc1_ref, part_ref) = rest[:6], rest[6:]
    channels = lift_ref.shape[1]
    pair = 2 * channels
    acc0_ref[...] = jnp.zeros_like(acc0_ref)
    acc1_ref[...] = jnp.zeros_like(acc1_ref)
    upper = lax.broadcasted_iota(jnp.int32, (1, pair), 1) >= channels
    corner_z = jnp.where(upper, 1.0, 0.0)
    lane_bit = lax.broadcasted_iota(jnp.int32, (128, pair), 1) // channels

    def twice(values):
        return jnp.concatenate([values, values], axis=1)

    lift = jnp.concatenate([twice(lift_ref[...]), jnp.zeros((16, pair), F32)], axis=0).astype(BF)
    query = jnp.concatenate(
        [jnp.zeros((8, pair), F32), twice(query_ref[...]), jnp.zeros((8, pair), F32)], axis=0
    ).astype(BF)
    layers = []
    for k in range(2):
        inner_ref, bias_ref, outer_ref = nets[3 * k : 3 * k + 3]
        outer = outer_ref[...].astype(F32)
        blank = jnp.zeros_like(outer)
        both = jnp.concatenate(
            [jnp.concatenate([outer, blank], axis=1), jnp.concatenate([blank, outer], axis=1)], axis=0
        ).astype(BF)
        inner = [twice(inner_ref[i : i + 1, :]) for i in range(3)]
        layers.append((inner, twice(bias_ref[...]) + corner_z * inner[2], both))

    @pl.loop(0, count_ref[0])
    def _(index):
        slot = order_ref[index]
        points = jnp.transpose(pts_ref[slot], (1, 0))
        rounded = points.astype(BF)
        values = [
            jnp.dot(rounded, weight, preferred_element_type=F32).astype(BF).astype(F32)
            for weight in (lift, query)
        ]
        fraction = [jnp.broadcast_to(points[:, 12 + i : 13 + i], (128, pair)) for i in range(3)]
        bits = jnp.broadcast_to(points[:, 18:19], (128, pair)).astype(jnp.int32) >> lane_bit
        live = [((bits >> (2 * t)) & 1).astype(F32) for t in range(4)]
        for k in range(2):
            inner, start, both = layers[k]
            base = start - (fraction[0] * inner[0] + fraction[1] * inner[1] + fraction[2] * inner[2])
            for t in range(4):
                hidden = smooth(base + ((t // 2) * inner[0] + (t % 2) * inner[1])).astype(BF)
                out = lax.dot_general(hidden, both, NT, preferred_element_type=F32)
                out = (out * live[t]).astype(BF)
                if k == 1:
                    kept_ref[index, t] = out
                part_ref[:, 4 * k + t, :] = out.astype(F32) * values[k]

        @pl.loop(0, 128 // UNROLL)
        def _(group):
            for u in range(0, UNROLL, 2):
                place = group * UNROLL + u
                even, odd = cells_ref[slot, place], cells_ref[slot, place + 1]
                acc0_ref[even] += part_ref[place]
                acc1_ref[odd] += part_ref[place + 1]

    for row in range((GXD + 1) * GY):
        for k, out_ref in ((0, own_ref), (1, grad_ref)):
            total = None
            for t in range(4):
                source = row - (t // 2) * GY - t % 2
                if 0 <= source < GXD * GY:
                    for acc_ref in (acc0_ref, acc1_ref):
                        piece = acc_ref[source * GZ : (source + 1) * GZ, 4 * k + t, :]
                        total = piece if total is None else total + piece
            flat = jnp.transpose(total, (1, 0))
            flat = flat[0:channels] + pltpu.roll(flat[channels:], 1, 1)
            out_ref[:, row * GZ : (row + 1) * GZ] = flat.astype(out_ref.dtype)


def scatter_points(order, count, cells, pts, lift, query, *nets):
    channels = lift.shape[1]
    slots = pts.shape[0]
    smem = pl.BlockSpec(memory_space=pltpu.SMEM)
    vmem = pl.BlockSpec(memory_space=pltpu.VMEM)
    return pl.pallas_call(
        scatter_kernel,
        out_shape=[
            jax.ShapeDtypeStruct((channels, EXT), BF),
            jax.ShapeDtypeStruct((channels, EXT), F32),
            jax.ShapeDtypeStruct((slots, 4, 128, 2 * channels), BF),
        ],
        in_specs=[smem] * 3 + [vmem] * 9,
        out_specs=[vmem] * 3,
        scratch_shapes=[
            pltpu.VMEM((BASE, 8, 2 * channels), F32),
            pltpu.VMEM((BASE, 8, 2 * channels), F32),
            pltpu.VMEM((128, 8, 2 * channels), F32),
        ],
        compiler_params=pltpu.CompilerParams(vmem_limit_bytes=VMEM_LIMIT),
    )(order, count, cells, pts, lift, query, *nets)


def level_kernel(
    order_ref, count_ref, edge_ref, cells_ref, own_ref, left_ref, right_ref, grad_ref, kept_ref,
    weight_ref, bias_ref, out_w_ref, pred_ref, sg_ref, lz_ref, pre_ref, lat_ref, table_ref, got_ref,
    gp_ref, win_ref, sum_ref,
):
    channels = own_ref.shape[0]
    inside = jnp.where(edge_ref[0] > 0, 0.0, 1.0).astype(F32)
    z = lax.broadcasted_iota(jnp.int32, (channels, PLANE), 1) % GZ
    first, last = z == 0, z == GZ - 1
    lz_ref[...] = jnp.zeros_like(lz_ref)

    def put_plane(index, plane):
        start = index * PADDED + GZ
        lz_ref[channels : 2 * channels, start : start + PLANE] = plane.astype(BF)
        below = jnp.where(first, 0.0, pltpu.roll(plane, 1, 1))
        above = jnp.where(last, 0.0, pltpu.roll(plane, PLANE - 1, 1))
        lz_ref[0:channels, start : start + PLANE] = below.astype(BF)
        lz_ref[2 * channels :, start : start + PLANE] = above.astype(BF)

    def own(k):
        return own_ref[:, k * PLANE : (k + 1) * PLANE].astype(F32)

    put_plane(0, left_ref[:, 0:PLANE].astype(F32))
    put_plane(1, own(0) + left_ref[:, PLANE:].astype(F32))
    put_plane(2, own(1))
    put_plane(3, (own(2) + right_ref[:, 0:PLANE].astype(F32)) * inside)
    put_plane(4, right_ref[:, PLANE:].astype(F32))

    for x in range(3):
        total = None
        for a in range(3):
            start = (x + a) * PADDED
            terms = jnp.dot(
                weight_ref[a * 3 * channels : (a + 1) * 3 * channels, :],
                lz_ref[:, start : start + PADDED],
                preferred_element_type=F32,
            )
            for e in range(3):
                piece = terms[e * channels : (e + 1) * channels, e * GZ : e * GZ + PLANE]
                total = piece if total is None else total + piece
        pre = total + bias_ref[...]
        pre_ref[x] = pre
        out = smooth(pre)
        if x == 2:
            out = out * inside
        out = out.astype(BF).astype(F32)
        lat_ref[0:channels, x * PLANE : (x + 1) * PLANE] = out
        lat_ref[channels:, x * PLANE : (x + 1) * PLANE] = pltpu.roll(out, PLANE - 1, 1)
    for row in range((GXD + 1) * GY):
        flat = jnp.transpose(lat_ref[:, row * GZ : (row + 1) * GZ], (1, 0))
        for t in range(4):
            target = row - (t // 2) * GY - t % 2
            if 0 <= target < GXD * GY:
                table_ref[target * GZ : (target + 1) * GZ, t, :] = flat

    pred_ref[...] = jnp.zeros_like(pred_ref)
    out_w = jnp.concatenate([out_w_ref[...], out_w_ref[...]], axis=1).astype(BF)

    @pl.loop(0, count_ref[0])
    def _(index):
        slot = order_ref[index]

        @pl.loop(0, 128 // UNROLL)
        def _(group):
            for u in range(UNROLL):
                place = group * UNROLL + u
                got_ref[place] = table_ref[cells_ref[slot, place]]

        queried = None
        for t in range(4):
            term = got_ref[:, t, :] * kept_ref[index, t].astype(F32)
            queried = term if queried is None else queried + term
        pred_ref[slot] = lax.dot_general(out_w, queried.astype(BF), NT, preferred_element_type=F32)

    for x in range(3):
        grad = grad_ref[:, x * PLANE : (x + 1) * PLANE] * smooth_slope(pre_ref[x])
        if x == 2:
            grad = grad * inside
        gp_ref[0:channels, :] = jnp.where(last, 0.0, pltpu.roll(grad, PLANE - 1, 1)).astype(BF)
        gp_ref[channels : 2 * channels, :] = grad.astype(BF)
        gp_ref[2 * channels :, :] = jnp.where(first, 0.0, pltpu.roll(grad, 1, 1)).astype(BF)
        for k in range(9):
            start = (x + k // 3) * PADDED + (k % 3) * GZ
            win_ref[k * channels : (k + 1) * channels, :] = lz_ref[
                channels : 2 * channels, start : start + PLANE
            ]
        term = lax.dot_general(gp_ref[...], win_ref[...], NT, preferred_element_type=F32)
        if x == 0:
            sum_ref[...] = term
        else:
            sum_ref[...] += term
    for k in range(27):
        f, place = k % 3, k // 3
        sg_ref[:, k * channels : (k + 1) * channels] = sum_ref[
            f * channels : (f + 1) * channels, place * channels : (place + 1) * channels
        ].astype(BF)


def level(order, count, edge, cells, own, left, right, grad, kept, weight, bias, out_w):
    channels = own.shape[0]
    slots = cells.shape[0]
    smem = pl.BlockSpec(memory_space=pltpu.SMEM)
    vmem = pl.BlockSpec(memory_space=pltpu.VMEM)
    return pl.pallas_call(
        level_kernel,
        out_shape=[
            jax.ShapeDtypeStruct((slots, out_w.shape[0], 128), F32),
            jax.ShapeDtypeStruct((channels, 27 * channels), BF),
        ],
        in_specs=[smem] * 4 + [vmem] * 8,
        out_specs=[vmem] * 2,
        scratch_shapes=[
            pltpu.VMEM((3 * channels, 5 * PADDED), BF),
            pltpu.VMEM((3, channels, PLANE), F32),
            pltpu.VMEM((2 * channels, EXT), F32),
            pltpu.VMEM((BASE, 4, 2 * channels), F32),
            pltpu.VMEM((128, 4, 2 * channels), F32),
            pltpu.VMEM((3 * channels, PLANE), BF),
            pltpu.VMEM((9 * channels, PLANE), BF),
            pltpu.VMEM((3 * channels, 9 * channels), F32),
        ],
        compiler_params=pltpu.CompilerParams(vmem_limit_bytes=VMEM_LIMIT),
    )(order, count, edge, cells, own, left, right, grad, kept, weight, bias, out_w)


def shards(
    point_fraction, point_features, base_cell, corner_bits, owner_map, cotangent, lift_weight,
    encode_inner, encode_bias, encode_outer, stencil_weight, stencil_bias, decode_inner,
    decode_bias, decode_outer, output_weight,
):
    devices = lax.axis_size("gx")
    me = lax.axis_index("gx")
    slots = devices * CAP
    channels = lift_weight.shape[0]
    target = owner_map[:, 0]
    held = target.shape[0]
    matching = target[:, None] == target[None, :]
    earlier = jnp.arange(held)[None, :] < jnp.arange(held)[:, None]
    ranking = jnp.sum(jnp.logical_and(matching, earlier), axis=1)
    places = target * CAP + ranking
    pick = (places[:, None] == jnp.arange(slots)[None, :]).astype(BF)

    packed = jnp.concatenate(
        [
            point_features,
            cotangent,
            point_fraction,
            jnp.zeros((held, 1, 128), BF),
            (base_cell // GZ).astype(BF)[:, None],
            (base_cell % GZ).astype(BF)[:, None],
            corner_bits.astype(BF)[:, None],
            jnp.ones((held, 1, 128), BF),
            jnp.zeros((held, 4, 128), BF),
        ],
        axis=1,
    ).reshape(held, -1)
    sent = jnp.dot(pick.T, packed, preferred_element_type=F32).astype(BF)
    pts = lax.all_to_all(sent, "gx", split_axis=0, concat_axis=0, tiled=True)
    pts = pts.reshape(slots, 24, 128).astype(F32)

    active = pts[:, 19, 0] > 0.5
    before = jnp.arange(slots)[None, :] < jnp.arange(slots)[:, None]
    count = jnp.sum(active.astype(jnp.int32))
    ahead_on = jnp.sum((before & active[None, :]).astype(jnp.int32), axis=1)
    ahead_off = jnp.sum((before & ~active[None, :]).astype(jnp.int32), axis=1)
    place = jnp.where(active, ahead_on, count + ahead_off)
    order = jnp.sum(
        jnp.where(place[None, :] == jnp.arange(slots)[:, None], jnp.arange(slots)[None, :], 0), axis=1
    ).astype(jnp.int32)
    count = count.reshape(1)
    edge = (me == devices - 1).astype(jnp.int32).reshape(1)

    cells = (pts[:, 16] * GZ + pts[:, 17]).astype(jnp.int32)
    query = jnp.pad(output_weight.astype(F32), ((0, 4), (0, 0)))
    own, grad, kept = scatter_points(
        order, count, cells, pts, lift_weight.astype(F32).T, query,
        encode_inner.T, encode_bias[None], encode_outer, decode_inner.T, decode_bias[None], decode_outer,
    )
    up = [(i, i + 1) for i in range(devices - 1)]
    down = [(i + 1, i) for i in range(devices - 1)]
    left = lax.ppermute(own[:, PLANE:], "gx", up)
    right = lax.ppermute(own[:, :BASE], "gx", down)
    weight = (
        stencil_weight.reshape(9, 3, channels, channels)
        .transpose(0, 2, 1, 3)
        .reshape(9 * channels, 3 * channels)
    )
    predicted, terms = level(
        order, count, edge, cells, own, left, right, grad, kept, weight, stencil_bias[:, None], query
    )
    outc = output_weight.shape[0]
    predicted = predicted[:, :outc].astype(BF).reshape(devices, -1)
    payload = jnp.concatenate([predicted, terms.reshape(devices, -1)], axis=1)
    back = lax.all_to_all(payload, "gx", split_axis=0, concat_axis=0, tiled=True)
    split = CAP * outc * 128
    returned = back[:, :split].reshape(slots, outc * 128)
    answer = jnp.dot(pick, returned, preferred_element_type=F32).astype(BF).reshape(held, outc, 128)
    stencil_grad = jnp.sum(back[:, split:].astype(F32), axis=0).reshape(-1, 27 * channels)
    return answer, stencil_grad


def solution(mesh):
    points = P(("grp", "gx"), None, None)
    flat = P(("grp", "gx"), None)
    return jax.shard_map(
        shards,
        mesh=mesh,
        in_specs=(points, points, flat, flat, flat, points) + (P(),) * 10,
        out_specs=(points, flat),
        check_vma=False,
    )
```

```python
import functools

import jax
import jax.numpy as jnp
from jax import lax
from jax.experimental import pallas as pl
from jax.experimental.pallas import tpu as pltpu
from jax.sharding import PartitionSpec as P

CAP = 2
GXD = 2
GY = 16
GZ = 128
PLANE = GY * GZ
BASE = GXD * PLANE
EXT = (GXD + 1) * PLANE
PADDED = (GY + 2) * GZ
UNROLL = 16
ACCS = 2
BF = jnp.bfloat16
F32 = jnp.float32
NT = (((1,), (1,)), ((), ()))
VMEM_LIMIT = 60 * 1024 * 1024


def smooth(v):
    return 0.5 * v * (1.0 + jnp.tanh(v * (0.7978845608 + (0.7978845608 * 0.044715) * (v * v))))


def smooth_slope(v):
    square = v * v
    t = jnp.tanh(v * (0.7978845608 + (0.7978845608 * 0.044715) * square))
    inner = 0.7978845608 + (3.0 * 0.7978845608 * 0.044715) * square
    return 0.5 * (1.0 + t) + 0.5 * v * (1.0 - t * t) * inner


def scatter_kernel(
    active_ref, cells_ref, pts_ref, lift_ref, query_ref, *rest
):
    nets, (own_ref, grad_ref, kept_ref, part_ref), sums = rest[:6], rest[6:10], rest[10:]
    channels = lift_ref.shape[1]
    pair = 2 * channels
    for acc_ref in sums:
        acc_ref[...] = jnp.zeros_like(acc_ref)
    upper = lax.broadcasted_iota(jnp.int32, (1, pair), 1) >= channels
    corner_z = jnp.where(upper, 1.0, 0.0)
    lane_bit = lax.broadcasted_iota(jnp.int32, (128, pair), 1) // channels

    def twice(values):
        return jnp.concatenate([values, values], axis=1)

    lift = jnp.concatenate([twice(lift_ref[...]), jnp.zeros((16, pair), F32)], axis=0).astype(BF)
    query = jnp.concatenate(
        [jnp.zeros((8, pair), F32), twice(query_ref[...]), jnp.zeros((8, pair), F32)], axis=0
    ).astype(BF)
    layers = []
    for k in range(2):
        inner_ref, bias_ref, outer_ref = nets[3 * k : 3 * k + 3]
        outer = outer_ref[...].astype(F32)
        blank = jnp.zeros_like(outer)
        both = jnp.concatenate(
            [jnp.concatenate([outer, blank], axis=1), jnp.concatenate([blank, outer], axis=1)], axis=0
        ).astype(BF)
        inner = [twice(inner_ref[i : i + 1, :]) for i in range(3)]
        layers.append((inner, twice(bias_ref[...]) + corner_z * inner[2], both))

    @pl.loop(0, active_ref.shape[0])
    def _(slot):
      @pl.when(active_ref[slot] > 0)
      def _():
        points = jnp.transpose(pts_ref[slot], (1, 0))
        rounded = points.astype(BF)
        values = [
            jnp.dot(rounded, weight, preferred_element_type=F32).astype(BF).astype(F32)
            for weight in (lift, query)
        ]
        fraction = [jnp.broadcast_to(points[:, 12 + i : 13 + i], (128, pair)) for i in range(3)]
        bits = jnp.broadcast_to(points[:, 18:19], (128, pair)).astype(jnp.int32) >> lane_bit
        live = [((bits >> (2 * t)) & 1).astype(F32) for t in range(4)]
        for k in range(2):
            inner, start, both = layers[k]
            base = start - (fraction[0] * inner[0] + fraction[1] * inner[1] + fraction[2] * inner[2])
            for t in range(4):
                hidden = smooth(base + ((t // 2) * inner[0] + (t % 2) * inner[1])).astype(BF)
                out = lax.dot_general(hidden, both, NT, preferred_element_type=F32)
                out = (out * live[t]).astype(BF)
                if k == 1:
                    kept_ref[slot, t] = out
                part_ref[:, 4 * k + t, :] = out.astype(F32) * values[k]

        @pl.loop(0, 128 // UNROLL)
        def _(group):
            for u in range(UNROLL):
                place = group * UNROLL + u
                sums[u % ACCS][cells_ref[slot, place]] += part_ref[place]

    eye = jnp.where(
        lax.broadcasted_iota(jnp.int32, (pair, pair), 0) == lax.broadcasted_iota(jnp.int32, (pair, pair), 1),
        1.0,
        0.0,
    ).astype(BF)
    for row in range((GXD + 1) * GY):
        for k, out_ref in ((0, own_ref), (1, grad_ref)):
            total = None
            for t in range(4):
                source = row - (t // 2) * GY - t % 2
                if 0 <= source < GXD * GY:
                    for acc_ref in sums:
                        piece = acc_ref[source * GZ : (source + 1) * GZ, 4 * k + t, :]
                        total = piece if total is None else total + piece
            flat = lax.dot_general(eye, total.astype(BF), NT, preferred_element_type=F32)
            flat = flat[0:channels] + pltpu.roll(flat[channels:], 1, 1)
            out_ref[:, row * GZ : (row + 1) * GZ] = flat.astype(out_ref.dtype)


def scatter_points(active, cells, pts, lift, query, *nets):
    channels = lift.shape[1]
    slots = pts.shape[0]
    smem = pl.BlockSpec(memory_space=pltpu.SMEM)
    vmem = pl.BlockSpec(memory_space=pltpu.VMEM)
    return pl.pallas_call(
        scatter_kernel,
        out_shape=[
            jax.ShapeDtypeStruct((channels, EXT), BF),
            jax.ShapeDtypeStruct((channels, EXT), F32),
            jax.ShapeDtypeStruct((slots, 4, 128, 2 * channels), BF),
        ],
        in_specs=[smem] * 2 + [vmem] * 9,
        out_specs=[vmem] * 3,
        scratch_shapes=[
            pltpu.VMEM((128, 8, 2 * channels), F32),
        ]
        + [pltpu.VMEM((BASE, 8, 2 * channels), F32)] * ACCS,
        compiler_params=pltpu.CompilerParams(vmem_limit_bytes=VMEM_LIMIT),
    )(active, cells, pts, lift, query, *nets)


def level_kernel(
    active_ref, edge_ref, cells_ref, own_ref, left_ref, right_ref, grad_ref, kept_ref,
    weight_ref, bias_ref, out_w_ref, pred_ref, sg_ref, lz_ref, pre_ref, lat_ref, table_ref, got_ref,
    gp_ref, win_ref, sum_ref,
):
    channels = own_ref.shape[0]
    inside = jnp.where(edge_ref[0] > 0, 0.0, 1.0).astype(F32)
    z = lax.broadcasted_iota(jnp.int32, (channels, PLANE), 1) % GZ
    first, last = z == 0, z == GZ - 1
    lz_ref[...] = jnp.zeros_like(lz_ref)

    def put_plane(index, plane):
        start = index * PADDED + GZ
        lz_ref[channels : 2 * channels, start : start + PLANE] = plane.astype(BF)
        below = jnp.where(first, 0.0, pltpu.roll(plane, 1, 1))
        above = jnp.where(last, 0.0, pltpu.roll(plane, PLANE - 1, 1))
        lz_ref[0:channels, start : start + PLANE] = below.astype(BF)
        lz_ref[2 * channels :, start : start + PLANE] = above.astype(BF)

    def own(k):
        return own_ref[:, k * PLANE : (k + 1) * PLANE].astype(F32)

    put_plane(0, left_ref[:, 0:PLANE].astype(F32))
    put_plane(1, own(0) + left_ref[:, PLANE:].astype(F32))
    put_plane(2, own(1))
    put_plane(3, (own(2) + right_ref[:, 0:PLANE].astype(F32)) * inside)
    put_plane(4, right_ref[:, PLANE:].astype(F32))

    for x in range(3):
        total = None
        for a in range(3):
            start = (x + a) * PADDED
            terms = jnp.dot(
                weight_ref[a * 3 * channels : (a + 1) * 3 * channels, :],
                lz_ref[:, start : start + PADDED],
                preferred_element_type=F32,
            )
            for e in range(3):
                piece = terms[e * channels : (e + 1) * channels, e * GZ : e * GZ + PLANE]
                total = piece if total is None else total + piece
        pre = total + bias_ref[...]
        pre_ref[x] = pre
        out = smooth(pre)
        if x == 2:
            out = out * inside
        out = out.astype(BF).astype(F32)
        lat_ref[0:channels, x * PLANE : (x + 1) * PLANE] = out
        lat_ref[channels:, x * PLANE : (x + 1) * PLANE] = pltpu.roll(out, PLANE - 1, 1)
    for row in range((GXD + 1) * GY):
        flat = jnp.transpose(lat_ref[:, row * GZ : (row + 1) * GZ].astype(BF), (1, 0)).astype(F32)
        for t in range(4):
            target = row - (t // 2) * GY - t % 2
            if 0 <= target < GXD * GY:
                table_ref[target * GZ : (target + 1) * GZ, t, :] = flat

    pred_ref[...] = jnp.zeros_like(pred_ref)
    out_w = jnp.concatenate([out_w_ref[...], out_w_ref[...]], axis=1).astype(BF)

    @pl.loop(0, active_ref.shape[0])
    def _(slot):
      @pl.when(active_ref[slot] > 0)
      def _():

        @pl.loop(0, 128 // UNROLL)
        def _(group):
            for u in range(UNROLL):
                place = group * UNROLL + u
                got_ref[place] = table_ref[cells_ref[slot, place]]

        queried = None
        for t in range(4):
            term = got_ref[:, t, :] * kept_ref[slot, t].astype(F32)
            queried = term if queried is None else queried + term
        pred_ref[slot] = lax.dot_general(out_w, queried.astype(BF), NT, preferred_element_type=F32)

    for x in range(3):
        grad = grad_ref[:, x * PLANE : (x + 1) * PLANE] * smooth_slope(pre_ref[x])
        if x == 2:
            grad = grad * inside
        gp_ref[0:channels, :] = jnp.where(last, 0.0, pltpu.roll(grad, PLANE - 1, 1)).astype(BF)
        gp_ref[channels : 2 * channels, :] = grad.astype(BF)
        gp_ref[2 * channels :, :] = jnp.where(first, 0.0, pltpu.roll(grad, 1, 1)).astype(BF)
        for k in range(9):
            start = (x + k // 3) * PADDED + (k % 3) * GZ
            win_ref[k * channels : (k + 1) * channels, :] = lz_ref[
                channels : 2 * channels, start : start + PLANE
            ]
        term = lax.dot_general(gp_ref[...], win_ref[...], NT, preferred_element_type=F32)
        if x == 0:
            sum_ref[...] = term
        else:
            sum_ref[...] += term
    for k in range(27):
        f, place = k % 3, k // 3
        sg_ref[:, k * channels : (k + 1) * channels] = sum_ref[
            f * channels : (f + 1) * channels, place * channels : (place + 1) * channels
        ].astype(BF)


def level(active, edge, cells, own, left, right, grad, kept, weight, bias, out_w):
    channels = own.shape[0]
    slots = cells.shape[0]
    smem = pl.BlockSpec(memory_space=pltpu.SMEM)
    vmem = pl.BlockSpec(memory_space=pltpu.VMEM)
    return pl.pallas_call(
        level_kernel,
        out_shape=[
            jax.ShapeDtypeStruct((slots, out_w.shape[0], 128), F32),
            jax.ShapeDtypeStruct((channels, 27 * channels), BF),
        ],
        in_specs=[smem] * 3 + [vmem] * 8,
        out_specs=[vmem] * 2,
        scratch_shapes=[
            pltpu.VMEM((3 * channels, 5 * PADDED), BF),
            pltpu.VMEM((3, channels, PLANE), F32),
            pltpu.VMEM((2 * channels, EXT), F32),
            pltpu.VMEM((BASE, 4, 2 * channels), F32),
            pltpu.VMEM((128, 4, 2 * channels), F32),
            pltpu.VMEM((3 * channels, PLANE), BF),
            pltpu.VMEM((9 * channels, PLANE), BF),
            pltpu.VMEM((3 * channels, 9 * channels), F32),
        ],
        compiler_params=pltpu.CompilerParams(vmem_limit_bytes=VMEM_LIMIT),
    )(active, edge, cells, own, left, right, grad, kept, weight, bias, out_w)


def exchange_kernel(devices, src_ref, out_ref, send_sem, recv_sem, own_sem):
    me = lax.axis_index("gx")
    barrier = pltpu.get_barrier_semaphore()

    def greet(d, carry):
        pl.semaphore_signal(
            barrier, inc=1, device_id={"gx": lax.rem(me + d, devices)}, device_id_type=pl.DeviceIdType.MESH
        )
        return carry

    lax.fori_loop(1, devices, greet, 0)
    pl.semaphore_wait(barrier, devices - 1)
    own = pltpu.make_async_copy(src_ref.at[me], out_ref.at[me], own_sem)
    own.start()

    def sending(d):
        peer = lax.rem(me + d, devices)
        return pltpu.make_async_remote_copy(
            src_ref=src_ref.at[peer],
            dst_ref=out_ref.at[me],
            send_sem=send_sem.at[d],
            recv_sem=recv_sem.at[d],
            device_id={"gx": peer},
            device_id_type=pl.DeviceIdType.MESH,
        )

    def start(d, carry):
        sending(d).start()
        return carry

    def finish(d, carry):
        sending(d).wait()
        return carry

    lax.fori_loop(1, devices, start, 0)
    own.wait()
    lax.fori_loop(1, devices, finish, 0)


def exchange(blocks, collective_id):
    devices = blocks.shape[0]
    vmem = pl.BlockSpec(memory_space=pltpu.VMEM)
    return pl.pallas_call(
        functools.partial(exchange_kernel, devices),
        out_shape=jax.ShapeDtypeStruct(blocks.shape, blocks.dtype),
        in_specs=[vmem],
        out_specs=vmem,
        scratch_shapes=[
            pltpu.SemaphoreType.DMA((devices,)),
            pltpu.SemaphoreType.DMA((devices,)),
            pltpu.SemaphoreType.DMA,
        ],
        compiler_params=pltpu.CompilerParams(collective_id=collective_id, has_side_effects=True),
    )(blocks)


def shards(
    point_fraction, point_features, base_cell, corner_bits, owner_map, cotangent, lift_weight,
    encode_inner, encode_bias, encode_outer, stencil_weight, stencil_bias, decode_inner,
    decode_bias, decode_outer, output_weight,
):
    devices = lax.axis_size("gx")
    me = lax.axis_index("gx")
    slots = devices * CAP
    channels = lift_weight.shape[0]
    target = owner_map[:, 0]
    held = target.shape[0]
    matching = target[:, None] == target[None, :]
    earlier = jnp.arange(held)[None, :] < jnp.arange(held)[:, None]
    ranking = jnp.sum(jnp.logical_and(matching, earlier), axis=1)
    places = target * CAP + ranking
    pick = (places[:, None] == jnp.arange(slots)[None, :]).astype(BF)

    packed = jnp.concatenate(
        [
            point_features,
            cotangent,
            point_fraction,
            jnp.zeros((held, 1, 128), BF),
            (base_cell // GZ).astype(BF)[:, None],
            (base_cell % GZ).astype(BF)[:, None],
            corner_bits.astype(BF)[:, None],
            jnp.ones((held, 1, 128), BF),
            jnp.zeros((held, 12, 128), BF),
        ],
        axis=1,
    ).reshape(held, -1)
    sent = jnp.dot(pick.T, packed, preferred_element_type=F32).astype(BF)
    pts = exchange(sent.reshape(devices, CAP * 32, 128), 0)
    pts = pts.reshape(slots, 32, 128)[:, :24].astype(F32)

    active = pts[:, 19, 0].astype(jnp.int32)
    edge = (me == devices - 1).astype(jnp.int32).reshape(1)

    cells = (pts[:, 16] * GZ + pts[:, 17]).astype(jnp.int32)
    query = jnp.pad(output_weight.astype(F32), ((0, 4), (0, 0)))
    own, grad, kept = scatter_points(
        active, cells, pts, lift_weight.astype(F32).T, query,
        encode_inner.T, encode_bias[None], encode_outer, decode_inner.T, decode_bias[None], decode_outer,
    )
    up = [(i, i + 1) for i in range(devices - 1)]
    down = [(i + 1, i) for i in range(devices - 1)]
    left = lax.ppermute(own[:, PLANE:], "gx", up)
    right = lax.ppermute(own[:, :BASE], "gx", down)
    weight = (
        stencil_weight.reshape(9, 3, channels, channels)
        .transpose(0, 2, 1, 3)
        .reshape(9 * channels, 3 * channels)
    )
    predicted, terms = level(
        active, edge, cells, own, left, right, grad, kept, weight, stencil_bias[:, None], query
    )
    outc = output_weight.shape[0]
    predicted = predicted[:, :outc].astype(BF).reshape(devices, -1)
    payload = jnp.concatenate([predicted, terms.reshape(devices, -1)], axis=1)
    width = payload.shape[1]
    payload = jnp.pad(payload, ((0, 0), (0, -width % 2048)))
    back = exchange(payload.reshape(devices, -1, 128), 1).reshape(devices, -1)[:, :width]
    split = CAP * outc * 128
    returned = back[:, :split].reshape(slots, outc * 128)
    answer = jnp.dot(pick, returned, preferred_element_type=F32).astype(BF).reshape(held, outc, 128)
    stencil_grad = jnp.sum(back[:, split:].astype(F32), axis=0).reshape(-1, 27 * channels)
    return answer, stencil_grad


def solution(mesh):
    points = P(("grp", "gx"), None, None)
    flat = P(("grp", "gx"), None)
    return jax.shard_map(
        shards,
        mesh=mesh,
        in_specs=(points, points, flat, flat, flat, points) + (P(),) * 10,
        out_specs=(points, flat),
        check_vma=False,
    )
```
